32 devices in a mesh: dp: 8 (over z, x), tensor: 4 (over y, core).
Axes of the slice: x: 2, y: 2, z: 4, core: 2. Of those that a mesh axis runs over, the one named last changes fastest.
Arguments:
- cotangent: bfloat16 [4096, 4096], P(('dp', 'tensor')), may hold values from -6 to 6
- gate: bfloat16 [4096, 14336], P('dp', 'tensor'), may hold values from -8 to 8
- up: bfloat16 [4096, 14336], P('dp', 'tensor'), may hold values from -6 to 6
- w_down: bfloat16 [4, 14336, 4096], P(None, 'tensor', 'dp'), may hold values from -0.03125 to 0.03125
- language: int32 [8], replicated, may hold values from 0 to 3
Outputs:
- d_gate: bfloat16 [4096, 14336], P('dp', 'tensor')
- d_up: bfloat16 [4096, 14336], P('dp', 'tensor')
- d_weight: float32 [4, 14336, 4096], P(None, 'tensor', 'dp')
The draws below stay inside these ranges and needn't reach their ends.
All inputs are finite; a program needn't handle non-finite values.
Results may differ from the reference program's by a relative error of at most 0.0029.
Values may be sent and summed in bfloat16 or wider, within the bound.
A program may use at most 320 MiB of HBM per device.

```python
import jax
import jax.numpy as jnp
from jax import lax

D = 4096
FF = 14336
LANGS = 4
TOK_GRP = 512
GROUPS = 8
TOKENS = 4096
N_DP = 8


def touch_ends(values, key, least, largest):
    place = [jax.random.randint(jax.random.fold_in(key, axis), (), 0, length) for axis, length in enumerate(values.shape)]
    longest = values.shape.index(max(values.shape))
    next_to = place[:longest] + [(place[longest] + 1) % values.shape[longest]] + place[longest + 1:]
    return values.at[tuple(place)].set(least).at[tuple(next_to)].set(largest)


def block_scale(stream_key, dims, pieces, low, high):
    def one(position, shards_of):
        heights = jax.random.uniform(jax.random.fold_in(jax.random.fold_in(stream_key, 6), position), (shards_of,), jnp.float32, low / len(pieces), high / len(pieces))
        return jnp.repeat(jnp.exp(heights), dims[position] // shards_of).reshape((-1,) + (1,) * (len(dims) - position - 1))

    factor_of = one(*pieces[0])
    for cut in pieces[1:]:
        factor_of = factor_of * one(*cut)
    return factor_of


def normal_values(rng, dims, width, most, pieces=(), held_as=jnp.bfloat16):
    drawn = width * jax.random.normal(rng, dims, jnp.float32)
    if pieces:
        drawn = drawn * block_scale(rng, dims, pieces, -0.22, 0.18)
    return jnp.clip(drawn, -most, most).astype(held_as)


def setup_inputs(seed: int = 0) -> dict:
    key_of = jax.random.split(jax.random.key(seed), 6)
    cotangent = normal_values(key_of[0], (TOKENS, D), 1.0, 6.0, ((0, 32),))
    gate = normal_values(key_of[1], (TOKENS, FF), 2.0, 8.0, ((0, 8), (1, 4)))
    up = normal_values(key_of[2], (TOKENS, FF), 1.0, 6.0, ((0, 8), (1, 4)))
    w_down = normal_values(key_of[3], (LANGS, FF, D), (2 * FF) ** -0.5, 0.03125, ((1, 4), (2, 8)))
    language = touch_ends(jax.random.randint(key_of[4], (GROUPS,), 0, LANGS), jax.random.fold_in(key_of[4], 1), 0, LANGS - 1).astype(jnp.int32)
    return {"cotangent": cotangent, "gate": gate, "up": up, "w_down": w_down, "language": language}


def reference(cotangent, gate, up, w_down, language):
    cot3 = cotangent.reshape(N_DP, TOK_GRP, D)
    gate3 = gate.reshape(N_DP, TOK_GRP, FF)
    up3 = up.reshape(N_DP, TOK_GRP, FF)

    def step(accum, items):
        cot_g, gate_g, up_g, lang_g = items
        weights = w_down[lang_g]
        gate_f = gate_g.astype(jnp.float32)
        up_f = up_g.astype(jnp.float32)
        sig = jax.nn.sigmoid(gate_f)
        act = gate_f * sig
        hidden = (act * up_f).astype(jnp.bfloat16)
        d_hidden = jnp.dot(cot_g, weights.T, preferred_element_type=jnp.float32)
        d_up_g = (d_hidden * act).astype(jnp.bfloat16)
        d_gate_g = (d_hidden * up_f * sig * (1.0 + gate_f * (1.0 - sig))).astype(jnp.bfloat16)
        part = jnp.dot(hidden.T, cot_g, preferred_element_type=jnp.float32)
        accum = accum.at[lang_g].add(part)
        return accum, (d_gate_g, d_up_g)

    init = jnp.zeros((LANGS, FF, D), jnp.float32)
    d_weight, outs = lax.scan(step, init, (cot3, gate3, up3, language))
    d_gate = outs[0].reshape(N_DP * TOK_GRP, FF)
    d_up = outs[1].reshape(N_DP * TOK_GRP, FF)
    return d_gate, d_up, d_weight
```

```python
import functools

import jax
import jax.numpy as jnp
from jax import lax
from jax.experimental import pallas as pl
from jax.experimental.pallas import tpu as pltpu
from jax.sharding import PartitionSpec as P

NZ = 4


def weight_kernel(slots, lang_ref, group_ref, cot_ref, *refs):
    out_ref = refs[slots]
    out_ref[...] = jnp.zeros_like(out_ref)
    for s in range(slots):
        term = lax.dot_general(
            refs[s][...],
            cot_ref[group_ref[s]],
            (((0,), (0,)), ((), ())),
            preferred_element_type=jnp.float32,
        )
        out_ref[lang_ref[s]] += term


def weight_grad(langs, slot_lang, slot_group, cot, hiddens):
    slots = len(hiddens)
    tok, ff = hiddens[0].shape
    feat = cot.shape[2]
    tile = ff // 7
    return pl.pallas_call(
        functools.partial(weight_kernel, slots),
        out_shape=jax.ShapeDtypeStruct((langs, ff, feat), jnp.float32),
        grid_spec=pltpu.PrefetchScalarGridSpec(
            num_scalar_prefetch=2,
            grid=(ff // tile,),
            in_specs=[pl.BlockSpec(cot.shape, lambda i, *_: (0, 0, 0))]
            + [pl.BlockSpec((tok, tile), lambda i, *_: (0, i))] * slots,
            out_specs=pl.BlockSpec((langs, tile, feat), lambda i, *_: (0, i, 0)),
        ),
        compiler_params=pltpu.CompilerParams(vmem_limit_bytes=48 << 20),
        cost_estimate=pl.CostEstimate(
            flops=2 * slots * tok * ff * feat,
            bytes_accessed=2 * slots * tok * (ff + feat) + 4 * langs * ff * feat,
            transcendentals=0,
        ),
    )(slot_lang, slot_group, cot, *hiddens)


def shards(cotangent, gate, up, w_down, language):
    dp = lax.axis_size("dp")
    nx = dp // NZ
    me = lax.axis_index("dp")
    z, x = me // nx, me % nx
    langs, ff, feat = w_down.shape
    rows = cotangent.shape[0]

    def from_z(value, k):
        pairs = [(((a + k) % NZ) * nx + b, a * nx + b) for a in range(NZ) for b in range(nx)]
        return lax.ppermute(value, "dp", pairs)

    def from_x(value, k):
        pairs = [(a * nx + (b + k) % nx, a * nx + b) for a in range(NZ) for b in range(nx)]
        return lax.ppermute(value, "dp", pairs)

    columns = [[a * nx + b for a in range(NZ)] for b in range(nx)]
    cot_plane = lax.all_to_all(
        cotangent.reshape(rows, NZ, nx * feat).transpose(1, 0, 2),
        "dp", split_axis=0, concat_axis=0, axis_index_groups=columns, tiled=True,
    )
    cot_plane = lax.all_gather(cot_plane, "tensor", axis=1, tiled=True)
    cot_mine = lax.all_to_all(
        cotangent.reshape(rows, dp, feat).transpose(1, 0, 2),
        "dp", split_axis=0, concat_axis=0, tiled=True,
    )
    cot_mine = lax.all_gather(cot_mine, "tensor", axis=1, tiled=True)

    gate_f = gate.astype(jnp.float32)
    up_f = up.astype(jnp.float32)
    sig = jax.nn.sigmoid(gate_f)
    act = gate_f * sig
    hidden = (act * up_f).astype(jnp.bfloat16)

    column_hidden = [hidden] + [from_z(hidden, k) for k in range(1, NZ)]
    all_hidden = list(column_hidden)
    slot = [(k, 0) for k in range(NZ)]
    for j in range(1, nx):
        for k in range(NZ):
            all_hidden.append(from_x(column_hidden[k], j))
            slot.append((k, j))
    slot_group = jnp.stack([((z + k) % NZ) * nx + (x + j) % nx for k, j in slot]).astype(jnp.int32)
    slot_lang = language[slot_group]

    def slab(group):
        return lax.dynamic_index_in_dim(w_down, language[group], 0, keepdims=False)

    def share(k):
        plane = (z + k) % NZ
        cot = lax.dynamic_index_in_dim(cot_plane, plane, 0, keepdims=False)
        total = None
        for j in range(nx):
            source = (x + j) % nx
            weights = slab(plane * nx + x)
            if j:
                weights = from_x(slab(plane * nx + (x - j) % nx), j)
            piece = lax.dynamic_slice_in_dim(cot, source * feat, feat, 1)
            term = lax.dot_general(
                piece, weights, (((1,), (1,)), ((), ())), preferred_element_type=jnp.float32
            )
            total = term if total is None else total + term
        return total

    received = [from_z(share(k).astype(jnp.bfloat16), NZ - k) for k in (2, 1, 3)]
    d_hidden = share(0)
    for term in received:
        d_hidden = d_hidden + term.astype(jnp.float32)

    d_up = (d_hidden * act).astype(jnp.bfloat16)
    d_gate = (d_hidden * up_f * sig * (1.0 + gate_f * (1.0 - sig))).astype(jnp.bfloat16)
    d_weight = weight_grad(langs, slot_lang, slot_group, cot_mine, all_hidden)
    return (d_gate, d_up, d_weight)


def solution(mesh):
    return jax.shard_map(
        shards,
        mesh=mesh,
        in_specs=(
            P(("dp", "tensor"), None),
            P("dp", "tensor"),
            P("dp", "tensor"),
            P(None, "tensor", "dp"),
            P(),
        ),
        out_specs=(P("dp", "tensor"), P("dp", "tensor"), P(None, "tensor", "dp")),
        check_vma=False,
    )
```

```python
import functools

import jax
import jax.numpy as jnp
from jax import lax
from jax.experimental import pallas as pl
from jax.experimental.pallas import tpu as pltpu
from jax.sharding import PartitionSpec as P

NZ = 4


def weight_kernel(depths, lang_ref, place_ref, cot_ref, *refs):
    out_ref = refs[-1]
    out_ref[...] = jnp.zeros_like(out_ref)
    s = 0
    for ref, depth in zip(refs, depths):
        for j in range(depth):
            term = lax.dot_general(
                ref[j],
                cot_ref[place_ref[s]],
                (((0,), (0,)), ((), ())),
                preferred_element_type=jnp.float32,
            )
            out_ref[lang_ref[s]] += term
            s += 1


def weight_grad(langs, ff, first, places, cot, hiddens, into=None):
    depths = [h.shape[0] for h in hiddens]
    tok, width = hiddens[0].shape[1:]
    feat = cot.shape[2]
    tile = ff // 7
    args = [*places, cot, *hiddens]
    in_specs = [pl.BlockSpec(cot.shape, lambda i, *_: (0, 0, 0))]
    in_specs += [pl.BlockSpec((d, tok, tile), lambda i, *_: (0, 0, i)) for d in depths]
    aliases = {}
    if into is not None:
        aliases = {len(args): 0}
        args.append(into)
        in_specs.append(pl.BlockSpec(memory_space=pl.ANY))
    return pl.pallas_call(
        functools.partial(weight_kernel, depths),
        out_shape=jax.ShapeDtypeStruct((langs, ff, feat), jnp.float32),
        grid_spec=pltpu.PrefetchScalarGridSpec(
            num_scalar_prefetch=2,
            grid=(width // tile,),
            in_specs=in_specs,
            out_specs=pl.BlockSpec((langs, tile, feat), lambda i, *_: (0, first + i, 0)),
        ),
        input_output_aliases=aliases,
        compiler_params=pltpu.CompilerParams(vmem_limit_bytes=48 << 20),
        cost_estimate=pl.CostEstimate(
            flops=2 * sum(depths) * tok * width * feat,
            bytes_accessed=2 * sum(depths) * tok * (width + feat) + 4 * langs * width * feat,
            transcendentals=0,
        ),
    )(*args)


def shards(cotangent, gate, up, w_down, language):
    dp = lax.axis_size("dp")
    nx = dp // NZ
    me = lax.axis_index("dp")
    z, x = me // nx, me % nx
    langs, ff, feat = w_down.shape
    rows = cotangent.shape[0]

    def from_z(value, k):
        pairs = [(((a + k) % NZ) * nx + b, a * nx + b) for a in range(NZ) for b in range(nx)]
        return lax.ppermute(value, "dp", pairs)

    def from_x(value, k):
        pairs = [(a * nx + (b + k) % nx, a * nx + b) for a in range(NZ) for b in range(nx)]
        return lax.ppermute(value, "dp", pairs)

    def over_z(value, moves):
        return lax.ppermute(
            value, "dp", [(a * nx + b, c * nx + b) for a, c in moves for b in range(nx)]
        )

    def gather_z(value):
        near = over_z(value, [(0, 1), (1, 0), (2, 3), (3, 2)])
        mid = over_z(value, [(1, 2), (2, 1)])
        far = over_z(near, [(1, 2), (2, 1)])
        mid_end = over_z(mid, [(1, 0), (2, 3)])
        far_end = over_z(far, [(1, 0), (2, 3)])
        inner = (z == 1) | (z == 2)
        second = jnp.where(inner, mid, mid_end)
        third = jnp.where(inner, far, far_end)
        return [value, near, second, third], (near, mid), (far, mid_end)

    plane_of = [z, z + 1 - 2 * (z % 2), jnp.where(z < 2, 2, 1), jnp.where(z < 2, 3, 0)]

    def slab(group):
        return lax.dynamic_index_in_dim(w_down, language[group], 0, keepdims=False)

    def features(value, first, count):
        return lax.dynamic_slice_in_dim(value, first * feat, count * feat, value.ndim - 1)

    cot_rows = [features(cotangent, (z - k) % NZ * nx, nx) for k in range(NZ)]
    cot_rows = [from_z(c, k) if k else c for k, c in enumerate(cot_rows)]
    cot_own = [features(jnp.stack(cot_rows), (x - j) % nx, 1) for j in range(nx)]
    cot_own = [from_x(c, j) if j else c for j, c in enumerate(cot_own)]

    order = (2, 1, 3, 0)
    sent = {
        (k, j): slab((z + k) % NZ * nx + (x - j) % nx) for k in order for j in range(1, nx)
    }
    gate_f = gate.astype(jnp.float32)
    up_f = up.astype(jnp.float32)
    sig = jax.nn.sigmoid(gate_f)
    act = gate_f * sig
    hidden = (act * up_f).astype(jnp.bfloat16)
    sent, hidden = lax.optimization_barrier((sent, hidden))

    late = 2 * (ff // 7)
    late_hidden = hidden[:, ff - late :]
    late_column = jnp.stack([late_hidden] + [from_x(late_hidden, j) for j in range(1, nx)])
    crossed = {key: from_x(value, key[1]) for key, value in sent.items()}
    early, early_one, early_two = gather_z(hidden[None, :, : ff - late])
    lates, late_one, late_two = gather_z(late_column)

    cot_plane = lax.all_gather(jnp.stack(cot_rows), "tensor", axis=1, tiled=True)
    cot_mine = lax.all_gather(jnp.concatenate(cot_own), "tensor", axis=1, tiled=True)

    def share(k, after):
        plane = (z + k) % NZ
        cot, _ = lax.optimization_barrier((cot_plane[k], after))
        total = None
        for j in range(nx):
            source = (x + j) % nx
            weights = crossed[k, j] if j else slab(plane * nx + x)
            piece = features(cot, source, 1)
            term = lax.dot_general(
                piece, weights, (((1,), (1,)), ((), ())), preferred_element_type=jnp.float32
            )
            total = term if total is None else total + term
        return total

    def send_back(k, after):
        return from_z(share(k, after).astype(jnp.bfloat16), NZ - k)

    received = [
        send_back(2, early_one),
        send_back(1, early_two),
        send_back(3, late_one),
    ]
    d_hidden = share(0, (late_two, received[0]))
    early[3], received[1] = lax.optimization_barrier((early[3], received[1]))

    hiddens = list(early)
    groups = [(p, 0) for p in plane_of]
    for j in range(1, nx):
        hiddens += [from_x(h, j) for h in early]
        groups += [(p, j) for p in plane_of]
    d_hidden, _ = lax.optimization_barrier((d_hidden, hiddens[: len(hiddens) - 2]))
    for term in received:
        d_hidden = d_hidden + term.astype(jnp.float32)
    d_up = (d_hidden * act).astype(jnp.bfloat16)
    d_gate = (d_hidden * up_f * sig * (1.0 + gate_f * (1.0 - sig))).astype(jnp.bfloat16)

    late_groups = [(p, j) for p in plane_of for j in range(nx)]

    def places(slots):
        lang = language[jnp.stack([p * nx + (x + j) % nx for p, j in slots])]
        return lang, jnp.stack([j * NZ + (p - z) % NZ for p, j in slots]).astype(jnp.int32)

    d_weight = weight_grad(langs, ff, 5, places(late_groups), cot_mine, lates)
    d_weight = weight_grad(langs, ff, 0, places(groups), cot_mine, hiddens, d_weight)
    return (d_gate, d_up, d_weight)


def solution(mesh):
    return jax.shard_map(
        shards,
        mesh=mesh,
        in_specs=(
            P(("dp", "tensor"), None),
            P("dp", "tensor"),
            P("dp", "tensor"),
            P(None, "tensor", "dp"),
            P(),
        ),
        out_specs=(P("dp", "tensor"), P("dp", "tensor"), P(None, "tensor", "dp")),
        check_vma=False,
    )
```

```python
import functools

import jax
import jax.numpy as jnp
from jax import lax
from jax.experimental import pallas as pl
from jax.experimental.pallas import tpu as pltpu
from jax.sharding import PartitionSpec as P

NZ = 4


def weight_kernel(depths, lang_ref, place_ref, cot_ref, *refs):
    out_ref = refs[-1]
    out_ref[...] = jnp.zeros_like(out_ref)
    s = 0
    for ref, depth in zip(refs, depths):
        for j in range(depth):
            term = lax.dot_general(
                ref[j],
                cot_ref[place_ref[s]],
                (((0,), (0,)), ((), ())),
                preferred_element_type=jnp.float32,
            )
            out_ref[lang_ref[s]] += term
            s += 1


def weight_grad(langs, ff, first, places, cot, hiddens, into=None):
    depths = [h.shape[0] for h in hiddens]
    tok, width = hiddens[0].shape[1:]
    feat = cot.shape[2]
    tile = ff // 7
    args = [*places, cot, *hiddens]
    in_specs = [pl.BlockSpec(cot.shape, lambda i, *_: (0, 0, 0))]
    in_specs += [pl.BlockSpec((d, tok, tile), lambda i, *_: (0, 0, i)) for d in depths]
    aliases = {}
    if into is not None:
        aliases = {len(args): 0}
        args.append(into)
        in_specs.append(pl.BlockSpec(memory_space=pl.ANY))
    return pl.pallas_call(
        functools.partial(weight_kernel, depths),
        out_shape=jax.ShapeDtypeStruct((langs, ff, feat), jnp.float32),
        grid_spec=pltpu.PrefetchScalarGridSpec(
            num_scalar_prefetch=2,
            grid=(width // tile,),
            in_specs=in_specs,
            out_specs=pl.BlockSpec((langs, tile, feat), lambda i, *_: (0, first + i, 0)),
        ),
        input_output_aliases=aliases,
        compiler_params=pltpu.CompilerParams(vmem_limit_bytes=48 << 20),
        cost_estimate=pl.CostEstimate(
            flops=2 * sum(depths) * tok * width * feat,
            bytes_accessed=2 * sum(depths) * tok * (width + feat) + 4 * langs * width * feat,
            transcendentals=0,
        ),
    )(*args)


def shards(cotangent, gate, up, w_down, language):
    dp = lax.axis_size("dp")
    nx = dp // NZ
    me = lax.axis_index("dp")
    z, x = me // nx, me % nx
    langs, ff, feat = w_down.shape
    rows = cotangent.shape[0]

    def from_z(value, k):
        pairs = [(((a + k) % NZ) * nx + b, a * nx + b) for a in range(NZ) for b in range(nx)]
        return lax.ppermute(value, "dp", pairs)

    def from_x(value, k):
        pairs = [(a * nx + (b + k) % nx, a * nx + b) for a in range(NZ) for b in range(nx)]
        return lax.ppermute(value, "dp", pairs)

    def over_z(value, moves):
        return lax.ppermute(
            value, "dp", [(a * nx + b, c * nx + b) for a, c in moves for b in range(nx)]
        )

    def gather_z(value):
        near = over_z(value, [(0, 1), (1, 0), (2, 3), (3, 2)])
        mid = over_z(value, [(1, 2), (2, 1)])
        far = over_z(near, [(1, 2), (2, 1)])
        mid_end = over_z(mid, [(1, 0), (2, 3)])
        far_end = over_z(far, [(1, 0), (2, 3)])
        inner = (z == 1) | (z == 2)
        second = jnp.where(inner, mid, mid_end)
        third = jnp.where(inner, far, far_end)
        return [value, near, second, third], (near, mid), (far, mid_end)

    plane_of = [z, z + 1 - 2 * (z % 2), jnp.where(z < 2, 2, 1), jnp.where(z < 2, 3, 0)]

    def slab(group):
        return lax.dynamic_index_in_dim(w_down, language[group], 0, keepdims=False)

    def features(value, first, count):
        return lax.dynamic_slice_in_dim(value, first * feat, count * feat, value.ndim - 1)

    cot_rows = [features(cotangent, (z - k) % NZ * nx, nx) for k in range(NZ)]
    cot_rows = [from_z(c, k) if k else c for k, c in enumerate(cot_rows)]
    cot_own = [features(jnp.stack(cot_rows), (x - j) % nx, 1) for j in range(nx)]
    cot_own = [from_x(c, j) if j else c for j, c in enumerate(cot_own)]

    order = (2, 1, 3, 0)
    sent = {
        (k, j): slab((z + k) % NZ * nx + (x - j) % nx) for k in order for j in range(1, nx)
    }
    gate_f = gate.astype(jnp.float32)
    up_f = up.astype(jnp.float32)
    sig = jax.nn.sigmoid(gate_f)
    act = gate_f * sig
    hidden = (act * up_f).astype(jnp.bfloat16)
    sent, hidden = lax.optimization_barrier((sent, hidden))

    late = 2 * (ff // 7)
    late_hidden = hidden[:, ff - late :]
    late_column = jnp.stack([late_hidden] + [from_x(late_hidden, j) for j in range(1, nx)])
    crossed = {key: from_x(value, key[1]) for key, value in sent.items()}
    early, early_one, early_two = gather_z(hidden[None, :, : ff - late])
    lates, late_one, late_two = gather_z(late_column)

    cot_plane = lax.all_gather(jnp.stack(cot_rows), "tensor", axis=1, tiled=True)
    cot_mine = lax.all_gather(jnp.concatenate(cot_own), "tensor", axis=1, tiled=True)

    def share(k, after):
        plane = (z + k) % NZ
        cot, _ = lax.optimization_barrier((cot_plane[k], after))
        total = None
        for j in range(nx):
            source = (x + j) % nx
            weights = crossed[k, j] if j else slab(plane * nx + x)
            piece = features(cot, source, 1)
            term = lax.dot_general(
                piece, weights, (((1,), (1,)), ((), ())), preferred_element_type=jnp.float32
            )
            total = term if total is None else total + term
        return total

    def send_back(k, after):
        return from_z(share(k, after).astype(jnp.bfloat16), NZ - k)

    hiddens = list(early)
    groups = [(p, 0) for p in plane_of]
    own = [from_x(early[0], j) for j in range(1, nx)]
    swapped = [from_x(early[1], j) for j in range(1, nx)]
    received = [
        send_back(2, early_one),
        send_back(1, early_two),
        send_back(3, (late_one, own)),
    ]
    d_hidden = share(0, received[0])
    last, received[1], _ = lax.optimization_barrier((early[3], received[1], (late_two, swapped)))
    third = [from_x(early[2], j) for j in range(1, nx)]
    for j in range(1, nx):
        hiddens += [own[j - 1], swapped[j - 1], third[j - 1], from_x(last, j)]
        groups += [(p, j) for p in plane_of]
    d_hidden, _ = lax.optimization_barrier((d_hidden, third))
    for term in received:
        d_hidden = d_hidden + term.astype(jnp.float32)
    d_up = (d_hidden * act).astype(jnp.bfloat16)
    d_gate = (d_hidden * up_f * sig * (1.0 + gate_f * (1.0 - sig))).astype(jnp.bfloat16)

    late_groups = [(p, j) for p in plane_of for j in range(nx)]

    def places(slots):
        lang = language[jnp.stack([p * nx + (x + j) % nx for p, j in slots])]
        return lang, jnp.stack([j * NZ + (p - z) % NZ for p, j in slots]).astype(jnp.int32)

    d_weight = weight_grad(langs, ff, 5, places(late_groups), cot_mine, lates)
    d_weight = weight_grad(langs, ff, 0, places(groups), cot_mine, hiddens, d_weight)
    return (d_gate, d_up, d_weight)


def solution(mesh):
    return jax.shard_map(
        shards,
        mesh=mesh,
        in_specs=(
            P(("dp", "tensor"), None),
            P("dp", "tensor"),
            P("dp", "tensor"),
            P(None, "tensor", "dp"),
            P(),
        ),
        out_specs=(P("dp", "tensor"), P("dp", "tensor"), P(None, "tensor", "dp")),
        check_vma=False,
    )
```
